256 devices in a mesh: dp: 8 (over z_hi, x), mx: 4 (over z_lo), my: 8 (over y, core).
Axes of the slice: x: 4, y: 4, z: 8 (z_hi: 2, z_lo: 4; z = z_hi * 4 + z_lo), core: 2. Of those that a mesh axis runs over, the one named last changes fastest.
Arguments:
- tokens: bfloat16 [4096, 6144], P('dp', ('my', 'mx')), may hold values from -6 to 6
- w_in: bfloat16 [6144, 12288], P('my', 'mx'), may hold values from -0.078125 to 0.078125
- w_out: bfloat16 [12288, 6144], P('mx', 'my'), may hold values from -0.0546875 to 0.0546875
- cotangent: bfloat16 [4096, 6144], P('dp', ('my', 'mx')), may hold values from -6 to 6
Outputs:
- mixed: bfloat16 [4096, 6144], P('dp', ('my', 'mx'))
- d_tokens: bfloat16 [4096, 6144], P('dp', ('my', 'mx'))
- grad_in: bfloat16 [6144, 12288], P('my', ('mx', 'dp'))
- grad_out: bfloat16 [12288, 6144], P(('mx', 'dp'), 'my')
The draws below stay inside these ranges and needn't reach their ends.
All inputs are finite; a program needn't handle non-finite values.
Results may differ from the reference program's by a relative error of at most 0.0049.
Values may be sent and summed in bfloat16 or wider, within the bound.
A program may use at most 128 MiB of HBM per device.

```python
import jax
import jax.numpy as jnp
from jax import lax

D = 6144
FF = 12288
TOKENS = 4096


def steps_of(rng, extent, pieces, smallest, top_value):
    def one(axis_at, parts):
        heights = jax.random.uniform(jax.random.fold_in(jax.random.fold_in(rng, 6), axis_at), (parts,), jnp.float32, smallest / len(pieces), top_value / len(pieces))
        return jnp.repeat(jnp.exp(heights), extent[axis_at] // parts).reshape((-1,) + (1,) * (len(extent) - axis_at - 1))

    level = one(*pieces[0])
    for cut in pieces[1:]:
        level = level * one(*cut)
    return level


def gaussian(rng, shape, width, most, cuts=(), held_as=jnp.bfloat16):
    level = steps_of(rng, shape, cuts, -0.22, 0.18) if cuts else 1.0
    array = jax.random.normal(rng, shape, jnp.float32) * width * level
    return jnp.minimum(jnp.maximum(array, -most), most).astype(held_as)


def setup_inputs(seed: int = 0) -> dict:
    key_of = jax.random.split(jax.random.key(seed), 5)
    tokens = gaussian(key_of[0], (TOKENS, D), 1.0, 6.0, ((0, 8), (1, 32)))
    w_in = gaussian(key_of[1], (D, FF), D ** -0.5, 0.078125, ((0, 8), (1, 4)))
    w_out = gaussian(key_of[2], (FF, D), FF ** -0.5, 0.0546875, ((0, 4), (1, 8)))
    cotangent = gaussian(key_of[3], (TOKENS, D), 1.0, 6.0, ((0, 8), (1, 32)))
    return {"tokens": tokens, "w_in": w_in, "w_out": w_out, "cotangent": cotangent}


def gelu_parts(pre_act):
    root_half = 0.7071067811865476
    inv_root_two_pi = 0.3989422804014327
    cumul = 0.5 * (1.0 + lax.erf(pre_act * root_half))
    value = pre_act * cumul
    derivative = cumul + pre_act * jnp.exp(-0.5 * pre_act * pre_act) * inv_root_two_pi
    return value, derivative


def reference(tokens, w_in, w_out, cotangent):
    pre_act = jnp.dot(tokens, w_in, preferred_element_type=jnp.float32)
    value, derivative = gelu_parts(pre_act)
    hidden = value.astype(jnp.bfloat16)
    mixed = jnp.dot(hidden, w_out, preferred_element_type=jnp.float32).astype(jnp.bfloat16)
    d_hidden = jnp.dot(cotangent, w_out.T, preferred_element_type=jnp.float32)
    grad_pre = (d_hidden * derivative).astype(jnp.bfloat16)
    d_tokens = jnp.dot(grad_pre, w_in.T, preferred_element_type=jnp.float32).astype(jnp.bfloat16)
    grad_in = jnp.dot(tokens.T, grad_pre, preferred_element_type=jnp.float32).astype(jnp.bfloat16)
    grad_out = jnp.dot(hidden.T, cotangent, preferred_element_type=jnp.float32).astype(jnp.bfloat16)
    return (mixed, d_tokens, grad_in, grad_out)
```

```python
import jax
import jax.numpy as jnp
from jax import lax
from jax.experimental import pallas as pl
from jax.experimental.pallas import tpu as pltpu
from jax.sharding import Mesh
from jax.sharding import PartitionSpec as P

MESH = pl.DeviceIdType.MESH
BF = jnp.bfloat16
F32 = jnp.float32

TASKS = (
    (0, 0, 0, 3),
    (0, 1, 0, 3),
    (1, 0, 0, 3),
    (1, 1, 0, 1),
    (1, 1, 1, 1),
    (1, 1, 2, 1),
)
LINKS = {"y+": (0.0244, 2.4), "y-": (0.0244, 2.4), "x+": (0.0244, 2.4), "x-": (0.0244, 2.4)}
LINKS.update({"z+": (0.0244, 2.4), "z-": (0.0244, 2.4), "c": (0.0037, 0.9)})


def gelu_parts(pre_act):
    root_half = 0.7071067811865476
    inv_root_two_pi = 0.3989422804014327
    cumul = 0.5 * (1.0 + lax.erf(pre_act * root_half))
    value = pre_act * cumul
    derivative = cumul + pre_act * jnp.exp(-0.5 * pre_act * pre_act) * inv_root_two_pi
    return (value, derivative)


def dot(left, right, dims):
    return lax.dot_general(left, right, ((dims[:1], dims[1:]), ((), ())), preferred_element_type=F32)


class Plan:
    def __init__(self):
        self.steps, self.copies = {}, {}

    def copy(self, name, link, kb, src, dst, landing):
        self.copies[name] = (link, kb, src, dst, landing)

    def step(self, name, needs, cost, body, sends=()):
        self.steps[name] = (tuple(needs), cost, body, tuple(sends))

    def order(self):
        started_by = {c: s for s, v in self.steps.items() for c in v[3]}
        users = {s: [] for s in self.steps}
        for s, (needs, _, _, _) in self.steps.items():
            for n in needs:
                if n in self.copies:
                    link, kb = self.copies[n][:2]
                    per_kb, latency = LINKS[link]
                    users[started_by[n]].append((s, latency + per_kb * kb))
                else:
                    users[n].append((s, 0.0))
        level = {}

        def height(s):
            if s not in level:
                level[s] = self.steps[s][1] + max([height(u) + d for u, d in users[s]], default=0.0)
            return level[s]

        now, done, free = 0.0, {}, {}
        todo, result = list(self.steps), []
        while todo:
            best = None
            for s in todo:
                if any(n not in done for n in self.steps[s][0]):
                    continue
                at = max([done[n] for n in self.steps[s][0]], default=0.0)
                key = (max(at, now), -height(s))
                if best is None or key < best[0]:
                    best = (key, s)
            (at, _), s = best
            now = at + self.steps[s][1]
            done[s] = now
            for c in self.steps[s][3]:
                now += 0.05
                link, kb = self.copies[c][:2]
                per_kb, latency = LINKS[link]
                free[link] = max(free.get(link, 0.0), now) + per_kb * kb
                done[c] = free[link] + latency
            todo.remove(s)
            result.append(s)
        self.estimate = now
        return result


def kernel(tok_in, cot_in, w_in_hbm, w_out_hbm, mix_out, dtok_out, gin_out, gout_out, *scratch):
    (act, w_in, w_out, w_sem, csnd, crcv, own, ysnd, yrcv, deriv, hid, xsnd, xrcv, xown, zacc, zsnd, zrcv, send_sem, recv_sem) = scratch
    zh, x, zl = lax.axis_index("zh"), lax.axis_index("x"), lax.axis_index("zl")
    y, c = lax.axis_index("y"), lax.axis_index("c")
    z = zh * 4 + zl

    def along(axis, by):
        if axis == "z":
            to = lax.rem(z + by + 8, 8)
            return {"zh": to // 4, "zl": lax.rem(to, 4)}
        return {axis: lax.rem(lax.axis_index(axis) + by + 4, 4)}

    targets = {a + s: along(a, 1 if s == "+" else -1) for a in "xyz" for s in "+-"}
    targets["c"] = {"c": 1 - c}

    plan = Plan()

    loads = []
    for j in range(3):
        for xx in range(4):
            at = pl.multiple_of(zh * 1536 + xx * 384 + j * 128, 128)
            part = pl.ds(xx * 128, 128)
            loads.append(pltpu.make_async_copy(w_in_hbm.at[:, pl.ds(at, 128)], w_in.at[j, :, part], w_sem.at[0, j, xx]))
            loads.append(pltpu.make_async_copy(w_out_hbm.at[pl.ds(at, 128), :], w_out.at[j, part, :], w_sem.at[1, j, xx]))
    for load in loads:
        load.start()
    barrier = pltpu.get_barrier_semaphore()
    for target in targets.values():
        pl.semaphore_signal(barrier, inc=1, device_id=target, device_id_type=MESH)
    pl.semaphore_wait(barrier, len(targets))

    def place(a, h, at, first=0, rows=192):
        at = lax.rem(at + 16, 8)
        row = pl.multiple_of(lax.rem(at, 4) * 192 + first, 32)
        return act.at[a, h, pl.ds(row, rows), pl.ds(pl.multiple_of((at // 4) * 256, 256), 256)]

    def gather(a, h):
        source = (tok_in, cot_in)[a]

        def begin():
            place(a, h, z)[...] = source[h]

        for s in range(4):
            for sign, d in ((1, "z+"), (-1, "z-")):
                first, rows = (0, 192) if s < 3 else ((0, 96) if sign == 1 else (96, 96))
                here = place(a, h, z - sign * s, first, rows)
                there = place(a, h, z - sign * (s + 1), first, rows)
                plan.copy(("g", a, h, s, d), d, rows * 0.5, here, here, there)
            needs = [("g", a, h, s - 1, d) for d in ("z+", "z-")] if s else []
            sends = [("g", a, h, s, d) for d in ("z+", "z-")]
            plan.step(("g", a, h, s), needs, 0.1, begin if s == 0 else None, sends)
        plan.step(("act", a, h), [("g", a, h, 3, d) for d in ("z+", "z-")], 0.0, None)

    for a in range(2):
        for h in range(2):
            gather(a, h)

    def wait_weights():
        for load in loads:
            load.wait()

    plan.step("weights", [("g", 0, 0, 2)], 0.1, wait_weights)

    def hidden_task(t):
        p, h, j0, nj = TASKS[t]
        js = range(j0, j0 + nj)
        cut = pl.ds(j0, nj)

        def product(j, row):
            if p == 0:
                return dot(w_in[j, :, pl.ds(row, 128)], act[0, h], (0, 0))
            return dot(w_out[j, pl.ds(row, 128), :], act[1, h], (1, 0))

        def other_half():
            def body(i, _):
                j, k = j0 + i // 2, lax.rem(i, 2)
                row = pl.multiple_of((1 - c) * 256 + k * 128, 128)
                csnd[p, h, j, pl.ds(pl.multiple_of(k * 128, 128), 128), :] = product(j, row).astype(BF)
                return 0

            lax.fori_loop(0, 2 * nj, body, 0)

        def own_half():
            def body(i, _):
                j, k = j0 + i // 2, lax.rem(i, 2)
                row = pl.multiple_of(c * 256 + k * 128, 128)
                own[h, j, pl.ds(pl.multiple_of(k * 128, 128), 128), :] = product(j, row)
                return 0

            lax.fori_loop(0, 2 * nj, body, 0)

        def mine(j, rel, half):
            row = pl.ds(pl.multiple_of(lax.rem(y + rel, 4) * 64 + half * 32, 32), 32)
            return own[h, j, row, :] + crcv[p, h, j, row, :].astype(F32)

        def first_sums():
            for j in js:
                for rel, half in ((2, 0), (2, 1), (1, 1), (3, 0)):
                    ysnd[p, h, j, rel - 1, half] = mine(j, rel, half).astype(BF)

        def relay_sums():
            for j in js:
                for rel, half in ((1, 0), (3, 1)):
                    total = mine(j, rel, half) + yrcv[p, h, j, 1, half].astype(F32)
                    ysnd[p, h, j, rel - 1, half] = total.astype(BF)

        def activate():
            for j in js:
                for half in range(2):
                    total = mine(j, 0, half) + yrcv[p, h, j, 0, half].astype(F32) + yrcv[p, h, j, 2, half].astype(F32)
                    keep = pl.ds(half * 32, 32)
                    if p == 0:
                        value, slope = gelu_parts(total)
                        deriv[h, j, keep, :] = slope
                    else:
                        value = total * deriv[h, j, keep, :]
                    row = pl.ds(pl.multiple_of(c * 256 + y * 64 + half * 32, 32), 32)
                    hid[p, h, j, row, :] = value.astype(BF)

        def piece(core, rel, first=0, rows=64):
            row = core * 256 + lax.rem(y + rel, 4) * 64 + first
            return hid.at[p, h, cut, pl.ds(pl.multiple_of(row, 32), rows), :]

        n = lambda *rest: ("h", t) + rest
        plan.copy(n("c"), "c", 256 * nj, csnd.at[p, h, cut], crcv.at[p, h, cut], crcv.at[p, h, cut])
        for rel, half, d in ((2, 0, "y+"), (2, 1, "y-"), (1, 1, "y+"), (3, 0, "y-"), (1, 0, "y+"), (3, 1, "y-")):
            src, dst = ysnd.at[p, h, cut, rel - 1, half], yrcv.at[p, h, cut, rel - 1, half]
            plan.copy(n("r", rel, half), d, 32 * nj, src, dst, dst)
        needs = [("act", p, h), "weights"] + ([n0 for n0 in fwd_done if p == 1])
        plan.step(n("other"), needs, 0.25 * nj, other_half, [n("c")])
        plan.step(n("own"), [n("other")], 0.25 * nj, own_half)
        plan.step(n("first"), [n("own"), n("c")], 0.15 * nj, first_sums, [n("r", 2, 0), n("r", 2, 1), n("r", 1, 1), n("r", 3, 0)])
        plan.step(n("relay"), [n("first"), n("r", 2, 0), n("r", 2, 1)], 0.1 * nj, relay_sums, [n("r", 1, 0), n("r", 3, 1)])
        plan.copy(n("a", "+"), "y+", 64 * nj, piece(c, 0), piece(c, 0), piece(c, 3))
        plan.copy(n("a", "-"), "y-", 64 * nj, piece(c, 0), piece(c, 0), piece(c, 1))
        plan.copy(n("f", "+"), "y+", 32 * nj, piece(c, 3, 0, 32), piece(c, 3, 0, 32), piece(c, 2, 0, 32))
        plan.copy(n("f", "-"), "y-", 32 * nj, piece(c, 1, 32, 32), piece(c, 1, 32, 32), piece(c, 2, 32, 32))
        for rel in range(4):
            plan.copy(n("k", rel), "c", 64 * nj, piece(c, rel), piece(c, rel), piece(1 - c, rel))
        plan.step(n("act"), [n("relay")] + [n("r", *k) for k in ((1, 1), (3, 0), (1, 0), (3, 1))], 0.2 * nj, activate, [n("a", "+"), n("a", "-"), n("k", 0)])
        plan.step(n("pass"), [n("a", "+"), n("a", "-")], 0.05, None, [n("f", "+"), n("f", "-"), n("k", 1), n("k", 3)])
        plan.step(n("last"), [n("f", "+"), n("f", "-")], 0.05, None, [n("k", 2)])
        plan.step(n("done"), [n("k", rel) for rel in range(4)], 0.0, None)

    fwd_done = []
    for t, task in enumerate(TASKS):
        if task[0] == 0:
            hidden_task(t)
    fwd_done = [("h", t, "act") for t, task in enumerate(TASKS) if task[0] == 0]
    for t, task in enumerate(TASKS):
        if task[0] == 1:
            hidden_task(t)

    def gradient(p, j):
        other = 1 - p
        slot = p * 3 + j

        def product(rel):
            row = pl.ds(pl.multiple_of(lax.rem(x + rel, 4) * 128, 128), 128)
            return sum(dot(hid[p, h, j, row, :], act[other, h], (1, 1)) for h in range(2))

        def multiply():
            def body(i, _):
                total = product(3 - i).astype(BF)
                xsnd[slot, 2 - i, 0] = total[:64]
                xsnd[slot, 2 - i, 1] = total[64:]
                return 0

            lax.fori_loop(0, 3, body, 0)

        def multiply_own():
            xown[slot] = product(0)

        def relay_sums():
            for rel, half in ((1, 0), (3, 1)):
                total = xsnd[slot, rel - 1, half].astype(F32) + xrcv[slot, 1, half].astype(F32)
                xsnd[slot, rel - 1, half] = total.astype(BF)

        def finish():
            for half in range(2):
                rows = pl.ds(half * 64, 64)
                xown[slot, rows, :] = xown[slot, rows, :] + xrcv[slot, 0, half].astype(F32) + xrcv[slot, 2, half].astype(F32)
            if p == 0:
                gout_out[pl.ds(j * 128, 128), :] = xown[slot].astype(BF)
            else:
                gin_out[:, pl.ds(j * 128, 128)] = xown[slot].T.astype(BF)

        n = lambda *rest: ("w", p, j) + rest
        for rel, half, d in ((2, 0, "x+"), (2, 1, "x-"), (1, 1, "x+"), (3, 0, "x-"), (1, 0, "x+"), (3, 1, "x-")):
            plan.copy(n("r", rel, half), d, 96, xsnd.at[slot, rel - 1, half], xrcv.at[slot, rel - 1, half], xrcv.at[slot, rel - 1, half])
        needs = [("act", other, h) for h in range(2)]
        needs += [("h", t, "done") for t, (q, h, j0, nj) in enumerate(TASKS) if q == p and j0 <= j < j0 + nj]
        plan.step(n("mul"), needs, 0.9, multiply, [n("r", 2, 0), n("r", 2, 1), n("r", 1, 1), n("r", 3, 0)])
        plan.step(n("own"), [n("mul")], 0.3, multiply_own)
        plan.step(n("relay"), [n("mul"), n("r", 2, 0), n("r", 2, 1)], 0.15, relay_sums, [n("r", 1, 0), n("r", 3, 1)])
        plan.step(n("end"), [n("own")] + [n("r", *k) for k in ((1, 1), (3, 0), (1, 0), (3, 1))], 0.3, finish)

    for p in range(2):
        for j in range(3):
            gradient(p, j)

    def result(p, h):
        def multiply():
            def body(i, _):
                row = pl.ds(pl.multiple_of(i * 256, 256), 256)
                total = None
                for j in range(3):
                    if p == 0:
                        term = dot(w_out[j, :, row], hid[0, h, j], (0, 0))
                    else:
                        term = dot(w_in[j, row, :], hid[1, h, j], (1, 0))
                    total = term if total is None else total + term
                zacc[p, h, row, :] = total
                return 0

            lax.fori_loop(0, 3, body, 0)

        def mine(rel, first=0, rows=192):
            at = lax.rem(z + rel, 8)
            row = pl.multiple_of(lax.rem(at, 4) * 192 + first, 32)
            return zacc[p, h, pl.ds(row, rows), pl.ds(pl.multiple_of((at // 4) * 256, 256), 256)]

        def first():
            zsnd[p, h, 0, 0, pl.ds(0, 96), :] = mine(4, 0, 96).astype(BF)
            zsnd[p, h, 1, 0, pl.ds(96, 96), :] = mine(4, 96, 96).astype(BF)

        def add(s):
            def body():
                for d, rel in ((0, 4 - s), (1, 4 + s)):
                    for half in range(2):
                        total = mine(rel, half * 96, 96)
                        rows = pl.ds(half * 96, 96)
                        if s > 1 or half == d:
                            total = total + zrcv[p, h, d, s - 1, rows, :].astype(F32)
                        zsnd[p, h, d, s, rows, :] = total.astype(BF)

            return body

        def finish():
            total = mine(0) + zrcv[p, h, 0, 3].astype(F32) + zrcv[p, h, 1, 3].astype(F32)
            (mix_out, dtok_out)[p][h] = total.astype(BF)

        n = lambda *rest: ("z", p, h) + rest
        for d, link in ((0, "z+"), (1, "z-")):
            for s in range(4):
                rows = pl.ds(0, 192) if s else pl.ds(d * 96, 96)
                plan.copy(n("r", s, d), link, 96 if s else 48, zsnd.at[p, h, d, s, rows], zrcv.at[p, h, d, s, rows], zrcv.at[p, h, d, s, rows])
        needs = [("h", t, "done") for t, (q, hh, _, _) in enumerate(TASKS) if q == p and hh == h]
        plan.step(n("mul"), needs, 1.2, multiply)
        plan.step(n(0), [n("mul")], 0.1, first, [n("r", 0, 0), n("r", 0, 1)])
        for s in range(1, 4):
            plan.step(n(s), [n("r", s - 1, 0), n("r", s - 1, 1)], 0.3, add(s), [n("r", s, 0), n("r", s, 1)])
        plan.step(n("end"), [n("r", 3, 0), n("r", 3, 1)], 0.2, finish)

    for p in range(2):
        for h in range(2):
            result(p, h)

    index = {name: i for i, name in enumerate(plan.copies)}
    waited, sent = set(), []

    def remote(name, landing):
        link, _, src, dst, there = plan.copies[name]
        i = index[name]
        src, dst = (there, there) if landing else (src, dst)
        return pltpu.make_async_remote_copy(src, dst, send_sem.at[i], recv_sem.at[i], device_id=targets[link], device_id_type=MESH)

    for name in plan.order():
        needs, _, body, sends = plan.steps[name]
        for need in needs:
            if need in plan.copies and need not in waited:
                remote(need, True).wait_recv()
                waited.add(need)
        if body is not None:
            body()
        for copy in sends:
            remote(copy, False).start()
            sent.append(copy)
    for copy in sent:
        remote(copy, False).wait_send()


def copies_in_all():
    return 32 + 15 * len(TASKS) + 36 + 32


def per_device(tokens, w_in, w_out, cotangent):
    def turned(a):
        return a.reshape(2, 256, 192).transpose(0, 2, 1)

    vmem, far = pl.BlockSpec(memory_space=pltpu.VMEM), pl.BlockSpec(memory_space=pl.ANY)
    copies = copies_in_all()
    mixed, d_tokens, grad_in, grad_out = pl.pallas_call(
        kernel,
        out_shape=(
            jax.ShapeDtypeStruct((2, 192, 256), BF),
            jax.ShapeDtypeStruct((2, 192, 256), BF),
            jax.ShapeDtypeStruct((768, 384), BF),
            jax.ShapeDtypeStruct((384, 768), BF),
        ),
        in_specs=[vmem, vmem, far, far],
        out_specs=[vmem] * 4,
        scratch_shapes=[
            pltpu.VMEM((2, 2, 768, 512), BF),
            pltpu.VMEM((3, 768, 512), BF),
            pltpu.VMEM((3, 512, 768), BF),
            pltpu.SemaphoreType.DMA((2, 3, 4)),
            pltpu.VMEM((2, 2, 3, 256, 512), BF),
            pltpu.VMEM((2, 2, 3, 256, 512), BF),
            pltpu.VMEM((2, 3, 256, 512), F32),
            pltpu.VMEM((2, 2, 3, 3, 2, 32, 512), BF),
            pltpu.VMEM((2, 2, 3, 3, 2, 32, 512), BF),
            pltpu.VMEM((2, 3, 64, 512), F32),
            pltpu.VMEM((2, 2, 3, 512, 512), BF),
            pltpu.VMEM((6, 3, 2, 64, 768), BF),
            pltpu.VMEM((6, 3, 2, 64, 768), BF),
            pltpu.VMEM((6, 128, 768), F32),
            pltpu.VMEM((2, 2, 768, 512), F32),
            pltpu.VMEM((2, 2, 2, 4, 192, 256), BF),
            pltpu.VMEM((2, 2, 2, 4, 192, 256), BF),
            pltpu.SemaphoreType.DMA((copies,)),
            pltpu.SemaphoreType.DMA((copies,)),
        ],
        compiler_params=pltpu.CompilerParams(
            collective_id=0, has_side_effects=True, vmem_limit_bytes=62 * 2**20
        ),
        cost_estimate=pl.CostEstimate(flops=14_500_000_000, bytes_accessed=12_000_000, transcendentals=400_000),
    )(turned(tokens), turned(cotangent), w_in, w_out)

    def back(a):
        return a.transpose(0, 2, 1).reshape(512, 192)

    return (back(mixed), back(d_tokens), grad_in, grad_out)


def solution(mesh):
    split = Mesh(mesh.devices.reshape(2, 4, 4, 4, 2), ("zh", "x", "zl", "y", "c"))
    rows = P(("zh", "x"), ("y", "c", "zl"))
    return jax.shard_map(
        per_device,
        mesh=split,
        in_specs=(rows, P(("y", "c"), "zl"), P("zl", ("y", "c")), rows),
        out_specs=(rows, rows, P(("y", "c"), ("zl", "zh", "x")), P(("zl", "zh", "x"), ("y", "c"))),
        check_vma=False,
    )
```

```python
import jax
import jax.numpy as jnp
from jax import lax
from jax.experimental import pallas as pl
from jax.experimental.pallas import tpu as pltpu
from jax.sharding import Mesh
from jax.sharding import PartitionSpec as P

MESH = pl.DeviceIdType.MESH
BF = jnp.bfloat16
F32 = jnp.float32

TASKS = (
    (0, 0, 0, 3),
    (0, 1, 0, 3),
    (1, 0, 0, 3),
    (1, 1, 0, 1),
    (1, 1, 1, 1),
    (1, 1, 2, 1),
)
ORDER = (
    ("g", 0, 0, 0),
    ("g", 0, 1, 0),
    ("g", 0, 0, 1),
    ("g", 0, 1, 1),
    ("g", 0, 0, 2),
    "weights",
    ("g", 0, 1, 2),
    ("g", 0, 0, 3),
    ("g", 1, 0, 0),
    ("g", 0, 1, 3),
    ("g", 1, 1, 0),
    ("act", 0, 0),
    ("h", 0, "other"),
    ("h", 0, "own"),
    ("g", 1, 0, 1),
    ("act", 0, 1),
    ("h", 1, "other"),
    ("h", 0, "first"),
    ("g", 1, 1, 1),
    ("h", 1, "own"),
    ("g", 1, 0, 2),
    ("h", 1, "first"),
    ("h", 0, "relay"),
    ("g", 1, 1, 2),
    ("h", 1, "relay"),
    ("g", 1, 0, 3),
    ("g", 1, 1, 3),
    ("h", 0, "act"),
    ("act", 1, 1),
    ("h", 5, "other"),
    ("h", 4, "other"),
    ("act", 1, 0),
    ("h", 3, "other"),
    ("h", 1, "act"),
    ("h", 3, "own"),
    ("h", 2, "other"),
    ("h", 0, "pass"),
    ("h", 3, "first"),
    ("h", 4, "own"),
    ("h", 1, "pass"),
    ("h", 2, "own"),
    ("h", 2, "first"),
    ("h", 0, "last"),
    ("h", 0, "done"),
    ("h", 3, "relay"),
    ("z", 0, 0, "mul"),
    ("z", 0, 0, 0),
    ("h", 1, "last"),
    ("h", 5, "own"),
    ("h", 2, "relay"),
    ("h", 1, "done"),
    ("w", 0, 0, "mul"),
    ("z", 0, 0, 1),
    ("h", 4, "first"),
    ("h", 5, "first"),
    ("z", 0, 1, "mul"),
    ("z", 0, 1, 0),
    ("w", 0, 2, "mul"),
    ("h", 2, "act"),
    ("z", 0, 1, 1),
    ("w", 0, 0, "relay"),
    ("h", 3, "act"),
    ("w", 0, 1, "mul"),
    ("z", 0, 0, 2),
    ("w", 0, 2, "relay"),
    ("h", 5, "relay"),
    ("h", 4, "relay"),
    ("z", 0, 1, 2),
    ("h", 2, "pass"),
    ("z", 0, 0, 3),
    ("h", 3, "pass"),
    ("h", 5, "act"),
    ("w", 0, 0, "end"),
    ("h", 4, "act"),
    ("h", 2, "last"),
    ("h", 3, "last"),
    ("z", 0, 1, 3),
    ("w", 0, 1, "relay"),
    ("h", 5, "pass"),
    ("h", 3, "done"),
    ("h", 2, "done"),
    ("w", 1, 0, "mul"),
    ("h", 4, "pass"),
    ("z", 1, 0, "mul"),
    ("h", 5, "last"),
    ("z", 0, 0, "end"),
    ("h", 5, "done"),
    ("z", 0, 1, "end"),
    ("z", 1, 0, 0),
    ("h", 4, "last"),
    ("w", 1, 2, "mul"),
    ("h", 4, "done"),
    ("z", 1, 1, "mul"),
    ("z", 1, 1, 0),
    ("z", 1, 0, 1),
    ("w", 1, 1, "mul"),
    ("w", 0, 1, "end"),
    ("w", 0, 2, "end"),
    ("w", 1, 2, "relay"),
    ("z", 1, 1, 1),
    ("z", 1, 0, 2),
    ("w", 1, 0, "relay"),
    ("z", 1, 1, 2),
    ("w", 1, 1, "relay"),
    ("z", 1, 0, 3),
    ("w", 1, 2, "end"),
    ("z", 1, 1, 3),
    ("z", 1, 0, "end"),
    ("w", 1, 1, "end"),
    ("w", 1, 0, "end"),
    ("z", 1, 1, "end"),
)


def gelu_parts(pre_act):
    root_half = 0.7071067811865476
    inv_root_two_pi = 0.3989422804014327
    cumul = 0.5 * (1.0 + lax.erf(pre_act * root_half))
    value = pre_act * cumul
    derivative = cumul + pre_act * jnp.exp(-0.5 * pre_act * pre_act) * inv_root_two_pi
    return (value, derivative)


def dot(left, right, dims):
    return lax.dot_general(left, right, ((dims[:1], dims[1:]), ((), ())), preferred_element_type=F32)


class Plan:
    def __init__(self):
        self.steps, self.copies = {}, {}

    def copy(self, name, link, kb, src, dst, landing):
        self.copies[name] = (link, kb, src, dst, landing)

    def step(self, name, needs, cost, body, sends=()):
        self.steps[name] = (tuple(needs), cost, body, tuple(sends))


def kernel(tok_in, cot_in, w_in_hbm, w_out_hbm, mix_out, dtok_out, gin_out, gout_out, *scratch):
    (act, w_in, w_out, w_sem, csnd, crcv, own, ysnd, yrcv, deriv, hid, xsnd, xrcv, xown, xtmp, zacc, zsnd, zrcv, send_sem, recv_sem) = scratch
    zh, x, zl = lax.axis_index("zh"), lax.axis_index("x"), lax.axis_index("zl")
    y, c = lax.axis_index("y"), lax.axis_index("c")
    z = zh * 4 + zl

    def along(axis, by):
        if axis == "z":
            to = lax.rem(z + by + 8, 8)
            return {"zh": to // 4, "zl": lax.rem(to, 4)}
        return {axis: lax.rem(lax.axis_index(axis) + by + 4, 4)}

    targets = {a + s: along(a, 1 if s == "+" else -1) for a in "xyz" for s in "+-"}
    targets["c"] = {"c": 1 - c}

    plan = Plan()

    loads = []
    for j in range(3):
        for xx in range(4):
            at = pl.multiple_of(zh * 1536 + xx * 384 + j * 128, 128)
            part = pl.ds(xx * 128, 128)
            loads.append(pltpu.make_async_copy(w_in_hbm.at[:, pl.ds(at, 128)], w_in.at[j, :, part], w_sem.at[0, j, xx]))
            loads.append(pltpu.make_async_copy(w_out_hbm.at[pl.ds(at, 128), :], w_out.at[j, part, :], w_sem.at[1, j, xx]))
    for load in loads:
        load.start()
    barrier = pltpu.get_barrier_semaphore()
    for target in targets.values():
        pl.semaphore_signal(barrier, inc=1, device_id=target, device_id_type=MESH)
    pl.semaphore_wait(barrier, len(targets))

    def place(a, h, at, first=0, rows=192):
        at = lax.rem(at + 16, 8)
        row = pl.multiple_of(lax.rem(at, 4) * 192 + first, 32)
        return act.at[a, h, pl.ds(row, rows), pl.ds(pl.multiple_of((at // 4) * 256, 256), 256)]

    def gather(a, h):
        source = (tok_in, cot_in)[a]

        def begin():
            place(a, h, z)[...] = source[:, pl.ds(h * 256, 256)]

        for s in range(4):
            for sign, d in ((1, "z+"), (-1, "z-")):
                first, rows = (0, 192) if s < 3 else ((0, 96) if sign == 1 else (96, 96))
                here = place(a, h, z - sign * s, first, rows)
                there = place(a, h, z - sign * (s + 1), first, rows)
                plan.copy(("g", a, h, s, d), d, rows * 0.5, here, here, there)
            needs = [("g", a, h, s - 1, d) for d in ("z+", "z-")] if s else []
            sends = [("g", a, h, s, d) for d in ("z+", "z-")]
            plan.step(("g", a, h, s), needs, 0.1, begin if s == 0 else None, sends)
        plan.step(("act", a, h), [("g", a, h, 3, d) for d in ("z+", "z-")], 0.0, None)

    for a in range(2):
        for h in range(2):
            gather(a, h)

    def wait_weights():
        for load in loads:
            load.wait()

    plan.step("weights", [("g", 0, 0, 2)], 0.1, wait_weights)

    def hidden_task(t):
        p, h, j0, nj = TASKS[t]
        js = range(j0, j0 + nj)
        cut = pl.ds(j0, nj)

        def product(j, row):
            if p == 0:
                return dot(w_in[j, :, pl.ds(row, 256)], act[0, h], (0, 0))
            return dot(w_out[j, pl.ds(row, 256), :], act[1, h], (1, 0))

        def other_half():
            for j in js:
                csnd[p, h, j] = product(j, pl.multiple_of((1 - c) * 256, 256)).astype(BF)

        def own_half():
            for j in js:
                own[h, j] = product(j, pl.multiple_of(c * 256, 256))

        def mine(j, rel, half):
            row = pl.ds(pl.multiple_of(lax.rem(y + rel, 4) * 64 + half * 32, 32), 32)
            return own[h, j, row, :] + crcv[p, h, j, row, :].astype(F32)

        def first_sums():
            for j in js:
                for rel, half in ((2, 0), (2, 1), (1, 1), (3, 0)):
                    ysnd[p, h, j, rel - 1, half] = mine(j, rel, half).astype(BF)

        def relay_sums():
            for j in js:
                for rel, half in ((1, 0), (3, 1)):
                    total = mine(j, rel, half) + yrcv[p, h, j, 1, half].astype(F32)
                    ysnd[p, h, j, rel - 1, half] = total.astype(BF)

        def activate():
            for j in js:
                for half in range(2):
                    total = mine(j, 0, half) + yrcv[p, h, j, 0, half].astype(F32) + yrcv[p, h, j, 2, half].astype(F32)
                    keep = pl.ds(half * 32, 32)
                    if p == 0:
                        value, slope = gelu_parts(total)
                        deriv[h, j, keep, :] = slope
                    else:
                        value = total * deriv[h, j, keep, :]
                    row = pl.ds(pl.multiple_of(c * 256 + y * 64 + half * 32, 32), 32)
                    hid[p, h, j, row, :] = value.astype(BF)

        def piece(core, rel, first=0, rows=64):
            row = core * 256 + lax.rem(y + rel, 4) * 64 + first
            return hid.at[p, h, cut, pl.ds(pl.multiple_of(row, 32), rows), :]

        n = lambda *rest: ("h", t) + rest
        plan.copy(n("c"), "c", 256 * nj, csnd.at[p, h, cut], crcv.at[p, h, cut], crcv.at[p, h, cut])
        for rel, half, d in ((2, 0, "y+"), (2, 1, "y-"), (1, 1, "y+"), (3, 0, "y-"), (1, 0, "y+"), (3, 1, "y-")):
            src, dst = ysnd.at[p, h, cut, rel - 1, half], yrcv.at[p, h, cut, rel - 1, half]
            plan.copy(n("r", rel, half), d, 32 * nj, src, dst, dst)
        needs = [("act", p, h), "weights"] + ([n0 for n0 in fwd_done if p == 1])
        plan.step(n("other"), needs, 0.4 * nj, other_half, [n("c")])
        plan.step(n("own"), [n("other")], 0.4 * nj, own_half)
        plan.step(n("first"), [n("own"), n("c")], 0.1 * nj, first_sums, [n("r", 2, 0), n("r", 2, 1), n("r", 1, 1), n("r", 3, 0)])
        plan.step(n("relay"), [n("first"), n("r", 2, 0), n("r", 2, 1)], 0.06 * nj, relay_sums, [n("r", 1, 0), n("r", 3, 1)])
        plan.copy(n("a", "+"), "y+", 64 * nj, piece(c, 0), piece(c, 0), piece(c, 3))
        plan.copy(n("a", "-"), "y-", 64 * nj, piece(c, 0), piece(c, 0), piece(c, 1))
        plan.copy(n("f", "+"), "y+", 32 * nj, piece(c, 3, 0, 32), piece(c, 3, 0, 32), piece(c, 2, 0, 32))
        plan.copy(n("f", "-"), "y-", 32 * nj, piece(c, 1, 32, 32), piece(c, 1, 32, 32), piece(c, 2, 32, 32))
        for rel in range(4):
            plan.copy(n("k", rel), "c", 64 * nj, piece(c, rel), piece(c, rel), piece(1 - c, rel))
        plan.step(n("act"), [n("relay")] + [n("r", *k) for k in ((1, 1), (3, 0), (1, 0), (3, 1))], 0.12 * nj, activate, [n("a", "+"), n("a", "-"), n("k", 0)])
        plan.step(n("pass"), [n("a", "+"), n("a", "-")], 0.05, None, [n("f", "+"), n("f", "-"), n("k", 1), n("k", 3)])
        plan.step(n("last"), [n("f", "+"), n("f", "-")], 0.05, None, [n("k", 2)])
        plan.step(n("done"), [n("k", rel) for rel in range(4)], 0.0, None)

    fwd_done = []
    for t, task in enumerate(TASKS):
        if task[0] == 0:
            hidden_task(t)
    fwd_done = [("h", t, "act") for t, task in enumerate(TASKS) if task[0] == 0]
    for t, task in enumerate(TASKS):
        if task[0] == 1:
            hidden_task(t)

    def gradient(p, j):
        other = 1 - p
        slot = p * 3 + j

        def multiply():
            xtmp[...] = sum(dot(hid[p, h, j], act[other, h], (1, 1)) for h in range(2))
            for to in range(4):
                for half in range(2):
                    xsnd[slot, to, half] = xtmp[pl.ds(to * 128 + half * 64, 64), :].astype(BF)
            xown[slot] = xtmp[pl.ds(pl.multiple_of(x * 128, 128), 128), :]

        def relay_sums():
            for rel, half in ((1, 0), (3, 1)):
                to = lax.rem(x + rel, 4)
                total = xsnd[slot, to, half].astype(F32) + xrcv[slot, 1, half].astype(F32)
                xsnd[slot, to, half] = total.astype(BF)

        def finish():
            for half in range(2):
                rows = pl.ds(half * 64, 64)
                xown[slot, rows, :] = xown[slot, rows, :] + xrcv[slot, 0, half].astype(F32) + xrcv[slot, 2, half].astype(F32)
            if p == 0:
                gout_out[pl.ds(j * 128, 128), :] = xown[slot].astype(BF)
            else:
                gin_out[:, pl.ds(j * 128, 128)] = xown[slot].T.astype(BF)

        n = lambda *rest: ("w", p, j) + rest
        for rel, half, d in ((2, 0, "x+"), (2, 1, "x-"), (1, 1, "x+"), (3, 0, "x-"), (1, 0, "x+"), (3, 1, "x-")):
            plan.copy(n("r", rel, half), d, 96, xsnd.at[slot, lax.rem(x + rel, 4), half], xrcv.at[slot, rel - 1, half], xrcv.at[slot, rel - 1, half])
        needs = [("act", other, h) for h in range(2)]
        needs += [("h", t, "done") for t, (q, h, j0, nj) in enumerate(TASKS) if q == p and j0 <= j < j0 + nj]
        plan.step(n("mul"), needs, 1.2, multiply, [n("r", 2, 0), n("r", 2, 1), n("r", 1, 1), n("r", 3, 0)])
        plan.step(n("relay"), [n("mul"), n("r", 2, 0), n("r", 2, 1)], 0.15, relay_sums, [n("r", 1, 0), n("r", 3, 1)])
        plan.step(n("end"), [n("r", *k) for k in ((1, 1), (3, 0), (1, 0), (3, 1))], 0.25, finish)

    for p in range(2):
        for j in range(3):
            gradient(p, j)

    def result(p, h):
        def multiply():
            if p == 0:
                zacc[p, h] = sum(dot(w_out[j], hid[0, h, j], (0, 0)) for j in range(3))
            else:
                zacc[p, h] = sum(dot(w_in[j], hid[1, h, j], (1, 0)) for j in range(3))

        def mine(rel, first=0, rows=192):
            at = lax.rem(z + rel, 8)
            row = pl.multiple_of(lax.rem(at, 4) * 192 + first, 32)
            return zacc[p, h, pl.ds(row, rows), pl.ds(pl.multiple_of((at // 4) * 256, 256), 256)]

        def first():
            zsnd[p, h, 0, 0, pl.ds(0, 96), :] = mine(4, 0, 96).astype(BF)
            zsnd[p, h, 1, 0, pl.ds(96, 96), :] = mine(4, 96, 96).astype(BF)

        def add(s):
            def body():
                for d, rel in ((0, 4 - s), (1, 4 + s)):
                    for half in range(2):
                        total = mine(rel, half * 96, 96)
                        rows = pl.ds(half * 96, 96)
                        if s > 1 or half == d:
                            total = total + zrcv[p, h, d, s - 1, rows, :].astype(F32)
                        zsnd[p, h, d, s, rows, :] = total.astype(BF)

            return body

        def finish():
            total = mine(0) + zrcv[p, h, 0, 3].astype(F32) + zrcv[p, h, 1, 3].astype(F32)
            (mix_out, dtok_out)[p][:, pl.ds(h * 256, 256)] = total.astype(BF)

        n = lambda *rest: ("z", p, h) + rest
        for d, link in ((0, "z+"), (1, "z-")):
            for s in range(4):
                rows = pl.ds(0, 192) if s else pl.ds(d * 96, 96)
                plan.copy(n("r", s, d), link, 96 if s else 48, zsnd.at[p, h, d, s, rows], zrcv.at[p, h, d, s, rows], zrcv.at[p, h, d, s, rows])
        needs = [("h", t, "done") for t, (q, hh, _, _) in enumerate(TASKS) if q == p and hh == h]
        plan.step(n("mul"), needs, 1.45, multiply)
        plan.step(n(0), [n("mul")], 0.1, first, [n("r", 0, 0), n("r", 0, 1)])
        for s in range(1, 4):
            plan.step(n(s), [n("r", s - 1, 0), n("r", s - 1, 1)], 0.15, add(s), [n("r", s, 0), n("r", s, 1)])
        plan.step(n("end"), [n("r", 3, 0), n("r", 3, 1)], 0.15, finish)

    for p in range(2):
        for h in range(2):
            result(p, h)

    index = {name: i for i, name in enumerate(plan.copies)}
    waited, sent = set(), []

    def remote(name, landing):
        link, _, src, dst, there = plan.copies[name]
        i = index[name]
        src, dst = (there, there) if landing else (src, dst)
        return pltpu.make_async_remote_copy(src, dst, send_sem.at[i], recv_sem.at[i], device_id=targets[link], device_id_type=MESH)

    for name in ORDER:
        needs, _, body, sends = plan.steps[name]
        for need in needs:
            if need in plan.copies and need not in waited:
                remote(need, True).wait_recv()
                waited.add(need)
        if body is not None:
            body()
        for copy in sends:
            remote(copy, False).start()
            sent.append(copy)
        while len(sent) > 40:
            remote(sent.pop(0), False).wait_send()
    for copy in sent:
        remote(copy, False).wait_send()


def copies_in_all():
    return 32 + 15 * len(TASKS) + 36 + 32


def hand_over(*refs):
    for i in range(4):
        refs[4 + i][...] = refs[i][...]


def per_device(tokens, w_in, w_out, cotangent):
    vmem, far = pl.BlockSpec(memory_space=pltpu.VMEM), pl.BlockSpec(memory_space=pl.ANY)
    copies = copies_in_all()
    shapes = [jax.ShapeDtypeStruct(s, BF) for s in ((192, 512), (192, 512), (768, 384), (384, 768))]
    results = pl.pallas_call(
        kernel,
        out_shape=shapes,
        in_specs=[vmem, vmem, far, far],
        out_specs=[vmem] * 4,
        scratch_shapes=[
            pltpu.VMEM((2, 2, 768, 512), BF),
            pltpu.VMEM((3, 768, 512), BF),
            pltpu.VMEM((3, 512, 768), BF),
            pltpu.SemaphoreType.DMA((2, 3, 4)),
            pltpu.VMEM((2, 2, 3, 256, 512), BF),
            pltpu.VMEM((2, 2, 3, 256, 512), BF),
            pltpu.VMEM((2, 3, 256, 512), F32),
            pltpu.VMEM((2, 2, 3, 3, 2, 32, 512), BF),
            pltpu.VMEM((2, 2, 3, 3, 2, 32, 512), BF),
            pltpu.VMEM((2, 3, 64, 512), F32),
            pltpu.VMEM((2, 2, 3, 512, 512), BF),
            pltpu.VMEM((6, 4, 2, 64, 768), BF),
            pltpu.VMEM((6, 3, 2, 64, 768), BF),
            pltpu.VMEM((6, 128, 768), F32),
            pltpu.VMEM((512, 768), F32),
            pltpu.VMEM((2, 2, 768, 512), F32),
            pltpu.VMEM((2, 2, 2, 4, 192, 256), BF),
            pltpu.VMEM((2, 2, 2, 4, 192, 256), BF),
            pltpu.SemaphoreType.DMA((copies,)),
            pltpu.SemaphoreType.DMA((copies,)),
        ],
        compiler_params=pltpu.CompilerParams(
            collective_id=0, has_side_effects=True, vmem_limit_bytes=62 * 2**20
        ),
        cost_estimate=pl.CostEstimate(flops=14_500_000_000, bytes_accessed=12_000_000, transcendentals=400_000),
    )(tokens.T, cotangent.T, w_in, w_out)

    mixed, d_tokens, grad_in, grad_out = pl.pallas_call(
        hand_over,
        out_shape=shapes,
        in_specs=[vmem] * 4,
        out_specs=[vmem] * 4,
    )(*results)
    return (mixed.T, d_tokens.T, grad_in, grad_out)


def solution(mesh):
    split = Mesh(mesh.devices.reshape(2, 4, 4, 4, 2), ("zh", "x", "zl", "y", "c"))
    rows = P(("zh", "x"), ("y", "c", "zl"))
    return jax.shard_map(
        per_device,
        mesh=split,
        in_specs=(rows, P(("y", "c"), "zl"), P("zl", ("y", "c")), rows),
        out_specs=(rows, rows, P(("y", "c"), ("zl", "zh", "x")), P(("zl", "zh", "x"), ("y", "c"))),
        check_vma=False,
    )
```

```python
import jax
import jax.numpy as jnp
from jax import lax
from jax.experimental import pallas as pl
from jax.experimental.pallas import tpu as pltpu
from jax.sharding import Mesh
from jax.sharding import PartitionSpec as P

MESH = pl.DeviceIdType.MESH
BF = jnp.bfloat16
F32 = jnp.float32

TASKS = (
    (0, 0, 1, 0, 1),
    (0, 0, 1, 1, 1),
    (0, 0, 1, 2, 1),
    (0, 1, 1, 0, 1),
    (0, 1, 1, 1, 1),
    (0, 1, 1, 2, 1),
    (0, 2, 2, 0, 1),
    (0, 2, 2, 1, 1),
    (0, 2, 2, 2, 1),
    (1, 0, 2, 0, 1),
    (1, 2, 2, 0, 1),
    (1, 0, 2, 1, 1),
    (1, 2, 2, 1, 1),
    (1, 0, 2, 2, 1),
    (1, 2, 2, 2, 1),
)
SUMS = (((0, 2), (2, 2)), ((0, 1), (1, 1), (2, 1), (3, 1)))
FAR_GATHERS = ((0, 0),)
FAR_SUMS = ()
FAR_HIDDEN = ()
ORDER = (
    ("g", 0, 1, 0),
    ("g", 0, 0, 0),
    ("g", 0, 3, 0),
    ("g", 0, 1, 1),
    ("g", 0, 2, 0),
    ("g", 0, 0, 1),
    ("g", 0, 1, 2),
    ("g", 0, 2, 1),
    ("g", 0, 3, 1),
    "weights",
    ("act", 0, 0),
    ("h", 2, "other"),
    ("h", 0, "other"),
    ("h", 1, "other"),
    ("g", 0, 1, 3),
    ("h", 1, "own"),
    ("g", 1, 2, 0),
    ("h", 2, "own"),
    ("h", 2, "first"),
    ("h", 0, "own"),
    ("g", 0, 2, 2),
    ("h", 0, "first"),
    ("g", 0, 3, 2),
    ("g", 1, 3, 0),
    ("h", 1, "first"),
    ("act", 0, 1),
    ("h", 5, "other"),
    ("h", 3, "other"),
    ("h", 2, "relay"),
    ("h", 5, "own"),
    ("g", 1, 0, 0),
    ("h", 4, "other"),
    ("h", 0, "relay"),
    ("h", 5, "first"),
    ("h", 4, "own"),
    ("h", 3, "own"),
    ("h", 1, "relay"),
    ("g", 0, 2, 3),
    ("h", 3, "first"),
    ("g", 0, 3, 3),
    ("g", 1, 2, 1),
    ("h", 4, "first"),
    ("h", 2, "act"),
    ("g", 1, 3, 1),
    ("h", 5, "relay"),
    ("h", 0, "act"),
    ("g", 1, 1, 0),
    ("g", 1, 0, 1),
    ("h", 1, "act"),
    ("act", 0, 2),
    ("h", 3, "relay"),
    ("act", 0, 3),
    ("h", 8, "other"),
    ("h", 4, "relay"),
    ("h", 6, "other"),
    ("h", 8, "own"),
    ("h", 2, "pass"),
    ("h", 5, "act"),
    ("g", 1, 2, 2),
    ("h", 8, "first"),
    ("g", 1, 3, 2),
    ("h", 6, "own"),
    ("h", 7, "other"),
    ("h", 6, "first"),
    ("g", 1, 1, 1),
    ("g", 1, 0, 2),
    ("h", 2, "last"),
    ("h", 3, "act"),
    ("h", 7, "own"),
    ("h", 7, "first"),
    ("g", 1, 2, 3),
    ("h", 8, "relay"),
    ("h", 0, "pass"),
    ("g", 1, 3, 3),
    ("h", 6, "relay"),
    ("h", 5, "pass"),
    ("g", 1, 1, 2),
    ("h", 1, "pass"),
    ("h", 7, "relay"),
    ("g", 1, 0, 3),
    ("act", 1, 2),
    ("h", 4, "act"),
    ("act", 1, 3),
    ("h", 10, "other"),
    ("h", 8, "act"),
    ("h", 3, "pass"),
    ("h", 0, "last"),
    ("h", 6, "act"),
    ("g", 1, 1, 3),
    ("h", 14, "other"),
    ("h", 14, "own"),
    ("h", 7, "act"),
    ("h", 5, "last"),
    ("h", 1, "last"),
    ("act", 1, 0),
    ("h", 4, "pass"),
    ("h", 2, "done"),
    ("h", 10, "own"),
    ("h", 14, "first"),
    ("h", 12, "other"),
    ("h", 8, "pass"),
    ("act", 1, 1),
    ("h", 11, "other"),
    ("h", 13, "other"),
    ("h", 5, "done"),
    ("h", 6, "pass"),
    ("h", 9, "other"),
    ("h", 11, "own"),
    ("h", 7, "pass"),
    ("h", 10, "first"),
    ("h", 13, "own"),
    ("h", 14, "relay"),
    ("h", 13, "first"),
    ("h", 12, "own"),
    ("h", 9, "own"),
    ("h", 12, "first"),
    ("h", 0, "done"),
    ("h", 8, "last"),
    ("h", 6, "last"),
    ("h", 3, "last"),
    ("h", 7, "last"),
    ("h", 9, "first"),
    ("h", 8, "done"),
    ("h", 4, "last"),
    ("w", 0, 2, "mul"),
    ("h", 4, "done"),
    ("h", 10, "relay"),
    ("h", 7, "done"),
    ("h", 6, "done"),
    ("z", 0, 2, "mul"),
    ("z", 0, 2, 0),
    ("h", 13, "relay"),
    ("h", 3, "done"),
    ("h", 11, "first"),
    ("h", 12, "relay"),
    ("h", 14, "act"),
    ("h", 1, "done"),
    ("z", 0, 0, "mul"),
    ("z", 0, 0, 0),
    ("w", 0, 1, "mul"),
    ("z", 0, 2, 1),
    ("h", 13, "act"),
    ("h", 9, "relay"),
    ("h", 10, "act"),
    ("w", 0, 0, "mul"),
    ("h", 11, "relay"),
    ("z", 0, 0, 1),
    ("h", 14, "pass"),
    ("h", 12, "act"),
    ("w", 0, 1, "relay"),
    ("h", 13, "pass"),
    ("z", 0, 2, 2),
    ("w", 0, 2, "relay"),
    ("h", 9, "act"),
    ("h", 11, "act"),
    ("h", 10, "pass"),
    ("z", 0, 0, 2),
    ("h", 13, "last"),
    ("h", 12, "pass"),
    ("h", 14, "last"),
    ("w", 0, 0, "relay"),
    ("z", 0, 2, 3),
    ("h", 9, "pass"),
    ("h", 13, "done"),
    ("h", 14, "done"),
    ("w", 1, 2, "mul"),
    ("h", 11, "pass"),
    ("h", 10, "last"),
    ("z", 0, 0, 3),
    ("h", 12, "last"),
    ("h", 9, "last"),
    ("h", 10, "done"),
    ("h", 12, "done"),
    ("z", 1, 3, "mul"),
    ("z", 1, 2, "mul"),
    ("z", 1, 2, 0),
    ("z", 1, 3, 0),
    ("h", 11, "last"),
    ("h", 9, "done"),
    ("w", 1, 0, "mul"),
    ("h", 11, "done"),
    ("z", 1, 1, "mul"),
    ("z", 1, 1, 0),
    ("z", 1, 0, "mul"),
    ("z", 1, 0, 0),
    ("w", 1, 2, "relay"),
    ("z", 1, 2, 1),
    ("w", 0, 0, "end"),
    ("z", 1, 3, 1),
    ("w", 0, 2, "end"),
    ("w", 1, 1, "mul"),
    ("z", 1, 1, 1),
    ("z", 1, 0, 1),
    ("z", 0, 0, "end"),
    ("w", 0, 1, "end"),
    ("z", 1, 2, 2),
    ("z", 1, 3, 2),
    ("z", 1, 1, 2),
    ("z", 1, 0, 2),
    ("w", 1, 0, "relay"),
    ("z", 1, 2, 3),
    ("z", 1, 3, 3),
    ("z", 0, 2, "end"),
    ("w", 1, 1, "relay"),
    ("z", 1, 1, 3),
    ("z", 1, 0, 3),
    ("z", 1, 2, "end"),
    ("z", 1, 3, "end"),
    ("z", 1, 1, "end"),
    ("w", 1, 0, "end"),
    ("w", 1, 2, "end"),
    ("w", 1, 1, "end"),
    ("z", 1, 0, "end"),
)


def gelu_parts(pre_act):
    root_half = 0.7071067811865476
    inv_root_two_pi = 0.3989422804014327
    cumul = 0.5 * (1.0 + lax.erf(pre_act * root_half))
    value = pre_act * cumul
    derivative = cumul + pre_act * jnp.exp(-0.5 * pre_act * pre_act) * inv_root_two_pi
    return (value, derivative)


def dot(left, right, dims):
    return lax.dot_general(left, right, ((dims[:1], dims[1:]), ((), ())), preferred_element_type=F32)


class Plan:
    def __init__(self):
        self.steps, self.copies = {}, {}

    def copy(self, name, link, src, dst, landing):
        self.copies[name] = (link, src, dst, landing)

    def step(self, name, needs, body, sends=()):
        self.steps[name] = (tuple(needs), body, tuple(sends))


def kernel(tok_in, cot_in, w_in_hbm, w_out_hbm, mix_out, dtok_out, gin_out, gout_out, *scratch):
    (act, w_in, w_out, w_sem, csnd, crcv, own, ysnd, yrcv, deriv, hid, xsnd, xrcv, xown, xtmp, zacc, zsnd, zrcv, send_sem, recv_sem) = scratch
    zh, x, zl = lax.axis_index("zh"), lax.axis_index("x"), lax.axis_index("zl")
    y, c = lax.axis_index("y"), lax.axis_index("c")
    z = zh * 4 + zl

    def along(axis, by):
        if axis == "z":
            to = lax.rem(z + by + 8, 8)
            return {"zh": to // 4, "zl": lax.rem(to, 4)}
        return {axis: lax.rem(lax.axis_index(axis) + by + 4, 4)}

    targets = {a + s: along(a, 1 if s == "+" else -1) for a in "xyz" for s in "+-"}
    targets["c"] = {"c": 1 - c}
    if FAR_GATHERS or FAR_SUMS:
        targets.update({"z++": along("z", 2), "z--": along("z", -2)})
    if FAR_HIDDEN:
        targets["y2"] = along("y", 2)

    plan = Plan()

    loads = []
    for j in range(3):
        for xx in range(4):
            at = pl.multiple_of(zh * 1536 + xx * 384 + j * 128, 128)
            part = pl.ds(xx * 128, 128)
            loads.append(pltpu.make_async_copy(w_in_hbm.at[:, pl.ds(at, 128)], w_in.at[j, :, part], w_sem.at[0, j, xx]))
            loads.append(pltpu.make_async_copy(w_out_hbm.at[pl.ds(at, 128), :], w_out.at[j, part, :], w_sem.at[1, j, xx]))
    for load in loads:
        load.start()
    barrier = pltpu.get_barrier_semaphore()
    for target in targets.values():
        pl.semaphore_signal(barrier, inc=1, device_id=target, device_id_type=MESH)
    pl.semaphore_wait(barrier, len(targets))

    def place(a, q, at, first=0, rows=192):
        at = lax.rem(at + 16, 8)
        row = pl.multiple_of(lax.rem(at, 4) * 192 + first, 32)
        return act.at[a, q, pl.ds(row, rows), pl.ds(pl.multiple_of((at // 4) * 128, 128), 128)]

    def gather(a, q):
        source = (tok_in, cot_in)[a]

        def begin():
            place(a, q, z)[...] = source[:, pl.ds(q * 128, 128)]

        n = lambda *rest: ("g", a, q) + rest
        if (a, q) in FAR_GATHERS:
            for sign, d in ((1, "z+"), (-1, "z-")):
                near, far, half = z - sign, z - 2 * sign, (0 if sign == 1 else 96, 96)
                plan.copy(n(0, d), d + d[1], place(a, q, z), place(a, q, z), place(a, q, far))
                plan.copy(n(1, d), d, place(a, q, z), place(a, q, z), place(a, q, near))
                plan.copy(n(2, d), d + d[1], place(a, q, far, *half), place(a, q, far, *half), place(a, q, z - 4 * sign, *half))
                plan.copy(n(3, d), d, place(a, q, far), place(a, q, far), place(a, q, z - 3 * sign))
            plan.step(n(0), [], begin, [n(s, d) for s in (0, 1) for d in ("z+", "z-")])
            plan.step(n(1), [n(0, d) for d in ("z+", "z-")], None, [n(s, d) for s in (2, 3) for d in ("z+", "z-")])
            plan.step(("act", a, q), [n(s, d) for s in (1, 2, 3) for d in ("z+", "z-")], None)
            return
        for s in range(4):
            for sign, d in ((1, "z+"), (-1, "z-")):
                first, rows = (0, 192) if s < 3 else ((0, 96) if sign == 1 else (96, 96))
                here = place(a, q, z - sign * s, first, rows)
                there = place(a, q, z - sign * (s + 1), first, rows)
                plan.copy(n(s, d), d, here, here, there)
            needs = [n(s - 1, d) for d in ("z+", "z-")] if s else []
            plan.step(n(s), needs, begin if s == 0 else None, [n(s, d) for d in ("z+", "z-")])
        plan.step(("act", a, q), [n(3, d) for d in ("z+", "z-")], None)

    for a in range(2):
        for q in range(4):
            gather(a, q)

    def wait_weights():
        for load in loads:
            load.wait()

    plan.step("weights", [], wait_weights)

    def hidden_task(t):
        p, q0, nq, j0, nj = TASKS[t]
        units = [(q, j) for q in range(q0, q0 + nq) for j in range(j0, j0 + nj)]
        cut = (p, pl.ds(q0, nq), pl.ds(j0, nj))

        def product(q, j, row):
            if p == 0:
                return dot(w_in[j, :, pl.ds(row, 256)], act[0, q], (0, 0))
            return dot(w_out[j, pl.ds(row, 256), :], act[1, q], (1, 0))

        def other_half():
            for q, j in units:
                csnd[p, q, j] = product(q, j, pl.multiple_of((1 - c) * 256, 256)).astype(BF)

        def own_half():
            for q, j in units:
                own[q, j] = product(q, j, pl.multiple_of(c * 256, 256))

        def mine(q, j, rel, half):
            row = pl.ds(pl.multiple_of(lax.rem(y + rel, 4) * 64 + half * 32, 32), 32)
            return own[q, j, row, :] + crcv[p, q, j, row, :].astype(F32)

        def first_sums():
            for q, j in units:
                for rel, half in ((2, 0), (2, 1), (1, 1), (3, 0)):
                    ysnd[p, q, j, rel - 1, half] = mine(q, j, rel, half).astype(BF)

        def relay_sums():
            for q, j in units:
                for rel, half in ((1, 0), (3, 1)):
                    total = mine(q, j, rel, half) + yrcv[p, q, j, 1, half].astype(F32)
                    ysnd[p, q, j, rel - 1, half] = total.astype(BF)

        def activate():
            for q, j in units:
                for half in range(2):
                    total = mine(q, j, 0, half)
                    total = total + yrcv[p, q, j, 0, half].astype(F32) + yrcv[p, q, j, 2, half].astype(F32)
                    keep = pl.ds(half * 32, 32)
                    if p == 0:
                        value, slope = gelu_parts(total)
                        deriv[q, j, keep, :] = slope
                    else:
                        value = total * deriv[q, j, keep, :]
                    row = pl.ds(pl.multiple_of(c * 256 + y * 64 + half * 32, 32), 32)
                    hid[p, q, j, row, :] = value.astype(BF)

        def piece(core, rel, first=0, rows=64):
            row = core * 256 + lax.rem(y + rel, 4) * 64 + first
            return hid.at[(*cut, pl.ds(pl.multiple_of(row, 32), rows))]

        n = lambda *rest: ("h", t) + rest
        plan.copy(n("c"), "c", csnd.at[cut], crcv.at[cut], crcv.at[cut])
        for rel, half, d in ((2, 0, "y+"), (2, 1, "y-"), (1, 1, "y+"), (3, 0, "y-"), (1, 0, "y+"), (3, 1, "y-")):
            src, dst = ysnd.at[(*cut, rel - 1, half)], yrcv.at[(*cut, rel - 1, half)]
            plan.copy(n("r", rel, half), d, src, dst, dst)
        plan.step(n("other"), [("act", p, q) for q in range(q0, q0 + nq)] + ["weights"], other_half, [n("c")])
        plan.step(n("own"), [n("other")], own_half)
        plan.step(n("first"), [n("own"), n("c")], first_sums, [n("r", 2, 0), n("r", 2, 1), n("r", 1, 1), n("r", 3, 0)])
        plan.step(n("relay"), [n("first"), n("r", 2, 0), n("r", 2, 1)], relay_sums, [n("r", 1, 0), n("r", 3, 1)])
        plan.copy(n("a", "+"), "y+", piece(c, 0), piece(c, 0), piece(c, 3))
        plan.copy(n("a", "-"), "y-", piece(c, 0), piece(c, 0), piece(c, 1))
        far = t in FAR_HIDDEN
        for sign, rel, first in (("+", 3, 0), ("-", 1, 32)):
            here = piece(c, 0 if far else rel, first, 32)
            plan.copy(n("f", sign), "y2" if far else "y" + sign, here, here, piece(c, 2, first, 32))
        for rel in range(4):
            plan.copy(n("k", rel), "c", piece(c, rel), piece(c, rel), piece(1 - c, rel))
        plan.step(n("act"), [n("relay")] + [n("r", *k) for k in ((1, 1), (3, 0), (1, 0), (3, 1))], activate, [n("a", "+"), n("a", "-")] + [n("f", "+"), n("f", "-")] * far + [n("k", 0)])
        if far:
            plan.step(n("pass"), [n(a, b) for a in "af" for b in "+-"], None, [n("k", 1), n("k", 3), n("k", 2)])
        else:
            plan.step(n("pass"), [n("a", "+"), n("a", "-")], None, [n("f", "+"), n("f", "-"), n("k", 1), n("k", 3)])
            plan.step(n("last"), [n("f", "+"), n("f", "-")], None, [n("k", 2)])
        plan.step(n("done"), [n("k", rel) for rel in range(4)], None)

    for t in range(len(TASKS)):
        hidden_task(t)

    def hidden_ready(p, keep):
        return [("h", t, "done") for t, task in enumerate(TASKS) if task[0] == p and keep(*task[1:])]

    def gradient(p, j):
        other = 1 - p
        slot = p * 3 + j

        def multiply():
            xtmp[...] = sum(dot(hid[p, q, j], act[other, q], (1, 1)) for q in range(4))
            for to in range(4):
                for half in range(2):
                    xsnd[slot, to, half] = xtmp[pl.ds(to * 128 + half * 64, 64), :].astype(BF)
            xown[slot] = xtmp[pl.ds(pl.multiple_of(x * 128, 128), 128), :]

        def relay_sums():
            for rel, half in ((1, 0), (3, 1)):
                to = lax.rem(x + rel, 4)
                total = xsnd[slot, to, half].astype(F32) + xrcv[slot, 1, half].astype(F32)
                xsnd[slot, to, half] = total.astype(BF)

        def finish():
            for half in range(2):
                rows = pl.ds(half * 64, 64)
                xown[slot, rows, :] = xown[slot, rows, :] + xrcv[slot, 0, half].astype(F32) + xrcv[slot, 2, half].astype(F32)
            if p == 0:
                gout_out[pl.ds(j * 128, 128), :] = xown[slot].astype(BF)
            else:
                gin_out[:, pl.ds(j * 128, 128)] = xown[slot].T.astype(BF)

        n = lambda *rest: ("w", p, j) + rest
        for rel, half, d in ((2, 0, "x+"), (2, 1, "x-"), (1, 1, "x+"), (3, 0, "x-"), (1, 0, "x+"), (3, 1, "x-")):
            there = xrcv.at[slot, rel - 1, half]
            plan.copy(n("r", rel, half), d, xsnd.at[slot, lax.rem(x + rel, 4), half], there, there)
        needs = [("act", other, q) for q in range(4)] + hidden_ready(p, lambda q0, nq, j0, nj: j0 <= j < j0 + nj)
        plan.step(n("mul"), needs, multiply, [n("r", 2, 0), n("r", 2, 1), n("r", 1, 1), n("r", 3, 0)])
        plan.step(n("relay"), [n("mul"), n("r", 2, 0), n("r", 2, 1)], relay_sums, [n("r", 1, 0), n("r", 3, 1)])
        plan.step(n("end"), [n("r", *k) for k in ((1, 1), (3, 0), (1, 0), (3, 1))], finish)

    for p in range(2):
        for j in range(3):
            gradient(p, j)

    def result(p, q0, nq):
        qs, cut = range(q0, q0 + nq), pl.ds(q0, nq)

        def multiply():
            for q in qs:
                if p == 0:
                    zacc[p, q] = sum(dot(w_out[j], hid[0, q, j], (0, 0)) for j in range(3))
                else:
                    zacc[p, q] = sum(dot(w_in[j], hid[1, q, j], (1, 0)) for j in range(3))

        def mine(q, rel, first=0, rows=192):
            at = lax.rem(z + rel + 8, 8)
            row = pl.multiple_of(lax.rem(at, 4) * 192 + first, 32)
            return zacc[p, q, pl.ds(row, rows), pl.ds(pl.multiple_of((at // 4) * 128, 128), 128)]

        def first():
            for q in qs:
                zsnd[p, q, 0, 0, pl.ds(0, 96), :] = mine(q, 4, 0, 96).astype(BF)
                zsnd[p, q, 1, 0, pl.ds(96, 96), :] = mine(q, 4, 96, 96).astype(BF)

        def add(s):
            def body():
                for q in qs:
                    for d, rel in ((0, 4 - s), (1, 4 + s)):
                        for half in range(2):
                            total = mine(q, rel, half * 96, 96)
                            rows = pl.ds(half * 96, 96)
                            if s > 1 or half == d:
                                total = total + zrcv[p, q, d, s - 1, rows, :].astype(F32)
                            zsnd[p, q, d, s, rows, :] = total.astype(BF)

            return body

        def first_far():
            first()
            for q in qs:
                for d, sign in ((0, 1), (1, -1)):
                    zsnd[p, q, d, 1] = mine(q, 3 * sign).astype(BF)
                    zsnd[p, q, d, 3] = mine(q, sign).astype(BF)

        def add_far():
            for q in qs:
                for d, sign in ((0, 1), (1, -1)):
                    for half in range(2):
                        rows = pl.ds(half * 96, 96)
                        total = mine(q, 2 * sign, half * 96, 96) + zrcv[p, q, d, 1, rows, :].astype(F32)
                        if half == d:
                            total = total + zrcv[p, q, d, 0, rows, :].astype(F32)
                        zsnd[p, q, d, 2, rows, :] = total.astype(BF)

        is_far = (p, q0) in FAR_SUMS

        def finish():
            for q in qs:
                total = mine(q, 0)
                for d in range(2):
                    total = total + zrcv[p, q, d, 3].astype(F32)
                    if is_far:
                        total = total + zrcv[p, q, d, 2].astype(F32)
                (mix_out, dtok_out)[p][:, pl.ds(q * 128, 128)] = total.astype(BF)

        n = lambda *rest: ("z", p, q0) + rest
        for d, link in ((0, "z+"), (1, "z-")):
            for s in range(4):
                rows = pl.ds(0, 192) if s else pl.ds(d * 96, 96)
                there = zrcv.at[p, cut, d, s, rows]
                way = link + link[1] if is_far and s in (0, 2) else link
                plan.copy(n("r", s, d), way, zsnd.at[p, cut, d, s, rows], there, there)
        needs = hidden_ready(p, lambda a0, na, j0, nj: a0 < q0 + nq and q0 < a0 + na)
        plan.step(n("mul"), needs, multiply)
        if is_far:
            plan.step(n(0), [n("mul")], first_far, [n("r", s, d) for s in (0, 1, 3) for d in range(2)])
            plan.step(n(1), [n("r", s, d) for s in (0, 1) for d in range(2)], add_far, [n("r", 2, 0), n("r", 2, 1)])
            plan.step(n("end"), [n("r", s, d) for s in (2, 3) for d in range(2)], finish)
            return
        plan.step(n(0), [n("mul")], first, [n("r", 0, 0), n("r", 0, 1)])
        for s in range(1, 4):
            plan.step(n(s), [n("r", s - 1, 0), n("r", s - 1, 1)], add(s), [n("r", s, 0), n("r", s, 1)])
        plan.step(n("end"), [n("r", 3, 0), n("r", 3, 1)], finish)

    for p in range(2):
        for q0, nq in SUMS[p]:
            result(p, q0, nq)

    index = {name: i for i, name in enumerate(plan.copies)}
    waited, sent = set(), []

    def remote(name, landing):
        link, src, dst, there = plan.copies[name]
        i = index[name]
        src, dst = (there, there) if landing else (src, dst)
        return pltpu.make_async_remote_copy(src, dst, send_sem.at[i], recv_sem.at[i], device_id=targets[link], device_id_type=MESH)

    for name in ORDER:
        needs, body, sends = plan.steps[name]
        for need in needs:
            if need in plan.copies and need not in waited:
                remote(need, True).wait_recv()
                waited.add(need)
        if body is not None:
            body()
        for copy in sends:
            remote(copy, False).start()
            sent.append(copy)
        while len(sent) > 40:
            remote(sent.pop(0), False).wait_send()
    for copy in sent:
        remote(copy, False).wait_send()


def copies_in_all():
    return 64 + 15 * len(TASKS) + 36 + 8 * sum(len(groups) for groups in SUMS)


def hand_over(*refs):
    for i in range(4):
        refs[4 + i][...] = refs[i][...]


def per_device(tokens, w_in, w_out, cotangent):
    vmem, far = pl.BlockSpec(memory_space=pltpu.VMEM), pl.BlockSpec(memory_space=pl.ANY)
    copies = copies_in_all()
    shapes = [jax.ShapeDtypeStruct(s, BF) for s in ((192, 512), (192, 512), (768, 384), (384, 768))]
    results = pl.pallas_call(
        kernel,
        out_shape=shapes,
        in_specs=[vmem, vmem, far, far],
        out_specs=[vmem] * 4,
        scratch_shapes=[
            pltpu.VMEM((2, 4, 768, 256), BF),
            pltpu.VMEM((3, 768, 512), BF),
            pltpu.VMEM((3, 512, 768), BF),
            pltpu.SemaphoreType.DMA((2, 3, 4)),
            pltpu.VMEM((2, 4, 3, 256, 256), BF),
            pltpu.VMEM((2, 4, 3, 256, 256), BF),
            pltpu.VMEM((4, 3, 256, 256), F32),
            pltpu.VMEM((2, 4, 3, 3, 2, 32, 256), BF),
            pltpu.VMEM((2, 4, 3, 3, 2, 32, 256), BF),
            pltpu.VMEM((4, 3, 64, 256), F32),
            pltpu.VMEM((2, 4, 3, 512, 256), BF),
            pltpu.VMEM((6, 4, 2, 64, 768), BF),
            pltpu.VMEM((6, 3, 2, 64, 768), BF),
            pltpu.VMEM((6, 128, 768), F32),
            pltpu.VMEM((512, 768), F32),
            pltpu.VMEM((2, 4, 768, 256), F32),
            pltpu.VMEM((2, 4, 2, 4, 192, 128), BF),
            pltpu.VMEM((2, 4, 2, 4, 192, 128), BF),
            pltpu.SemaphoreType.DMA((copies,)),
            pltpu.SemaphoreType.DMA((copies,)),
        ],
        compiler_params=pltpu.CompilerParams(
            collective_id=0, has_side_effects=True, vmem_limit_bytes=62 * 2**20
        ),
        cost_estimate=pl.CostEstimate(flops=14_500_000_000, bytes_accessed=12_000_000, transcendentals=400_000),
    )(tokens.T, cotangent.T, w_in, w_out)

    mixed, d_tokens, grad_in, grad_out = pl.pallas_call(
        hand_over,
        out_shape=shapes,
        in_specs=[vmem] * 4,
        out_specs=[vmem] * 4,
    )(*results)
    return (mixed.T, d_tokens.T, grad_in, grad_out)


def solution(mesh):
    split = Mesh(mesh.devices.reshape(2, 4, 4, 4, 2), ("zh", "x", "zl", "y", "c"))
    rows = P(("zh", "x"), ("y", "c", "zl"))
    return jax.shard_map(
        per_device,
        mesh=split,
        in_specs=(rows, P(("y", "c"), "zl"), P("zl", ("y", "c")), rows),
        out_specs=(rows, rows, P(("y", "c"), ("zl", "zh", "x")), P(("zl", "zh", "x"), ("y", "c"))),
        check_vma=False,
    )
```

```python
import jax
import jax.numpy as jnp
from jax import lax
from jax.experimental import pallas as pl
from jax.experimental.pallas import tpu as pltpu
from jax.sharding import Mesh
from jax.sharding import PartitionSpec as P

MESH = pl.DeviceIdType.MESH
BF = jnp.bfloat16
F32 = jnp.float32

TASKS = (
    (0, 0, 1, 0, 1),
    (0, 0, 1, 1, 1),
    (0, 0, 1, 2, 1),
    (0, 1, 1, 0, 1),
    (0, 1, 1, 1, 1),
    (0, 1, 1, 2, 1),
    (0, 2, 2, 0, 1),
    (0, 2, 2, 1, 1),
    (0, 2, 2, 2, 1),
    (1, 0, 2, 0, 1),
    (1, 2, 2, 0, 1),
    (1, 0, 2, 1, 1),
    (1, 2, 2, 1, 1),
    (1, 0, 2, 2, 1),
    (1, 2, 2, 2, 1),
)
SUMS = (((0, 2), (2, 2)), ((0, 1), (1, 1), (2, 1), (3, 1)))
FAR_GATHERS = ((0, 0),)
FAR_SUMS = ()
FAR_HIDDEN = ()
ORDER = (
    3, 0, 13, 4, 8, 1, 5, 9, 14, 38, 2, 55, 39, 47, 6, 48, 28, 56, 57, 40, 10, 41, 15, 33, 49, 7, 79, 63, 58,
    80, 18, 71, 42, 81, 72, 64, 50, 11, 65, 16, 29, 73, 59, 34, 82, 43, 23, 19, 51, 12, 66, 17, 103, 74, 87,
    104, 60, 83, 30, 105, 35, 88, 95, 89, 24, 20, 61, 67, 96, 97, 31, 106, 44, 36, 90, 84, 25, 52, 98, 21, 32,
    75, 37, 119, 107, 68, 45, 91, 26, 151, 152, 99, 85, 53, 22, 76, 62, 120, 153, 135, 108, 27, 127, 143, 86,
    92, 111, 128, 100, 121, 144, 154, 145, 136, 112, 137, 46, 109, 93, 69, 101, 113, 110, 77, 165, 78, 122,
    102, 94, 183, 184, 146, 70, 129, 138, 155, 54, 177, 178, 162, 185, 147, 114, 123, 159, 130, 179, 156, 139,
    163, 148, 186, 166, 115, 131, 124, 180, 149, 140, 157, 160, 187, 116, 150, 158, 174, 132, 125, 181, 141,
    117, 126, 142, 207, 201, 202, 208, 133, 118, 168, 134, 195, 196, 189, 190, 175, 203, 161, 209, 167, 171,
    197, 191, 182, 164, 204, 210, 198, 192, 169, 205, 211, 188, 172, 199, 193, 206, 212, 200, 170, 176, 173,
    194,
)


def gelu_parts(pre_act):
    root_half = 0.7071067811865476
    inv_root_two_pi = 0.3989422804014327
    cumul = 0.5 * (1.0 + lax.erf(pre_act * root_half))
    value = pre_act * cumul
    derivative = cumul + pre_act * jnp.exp(-0.5 * pre_act * pre_act) * inv_root_two_pi
    return (value, derivative)


def dot(left, right, dims):
    return lax.dot_general(left, right, ((dims[:1], dims[1:]), ((), ())), preferred_element_type=F32)


class Plan:
    def __init__(self):
        self.steps, self.copies = {}, {}

    def copy(self, name, link, src, dst, landing):
        self.copies[name] = (link, src, dst, landing)

    def step(self, name, needs, body, sends=()):
        self.steps[name] = (tuple(needs), body, tuple(sends))


def kernel(tok_in, cot_in, w_in_hbm, w_out_hbm, mix_out, dtok_out, gin_out, gout_out, *scratch):
    (act, w_in, w_out, w_sem, csnd, crcv, own, ysnd, yrcv, deriv, hid, xsnd, xrcv, xown, xtmp, zacc, zsnd, zrcv, send_sem, recv_sem) = scratch
    zh, x, zl = lax.axis_index("zh"), lax.axis_index("x"), lax.axis_index("zl")
    y, c = lax.axis_index("y"), lax.axis_index("c")
    z = zh * 4 + zl

    def along(axis, by):
        if axis == "z":
            to = lax.rem(z + by + 8, 8)
            return {"zh": to // 4, "zl": lax.rem(to, 4)}
        return {axis: lax.rem(lax.axis_index(axis) + by + 4, 4)}

    targets = {a + s: along(a, 1 if s == "+" else -1) for a in "xyz" for s in "+-"}
    targets["c"] = {"c": 1 - c}
    if FAR_GATHERS or FAR_SUMS:
        targets.update({"z++": along("z", 2), "z--": along("z", -2)})
    if FAR_HIDDEN:
        targets["y2"] = along("y", 2)

    plan = Plan()

    loads = []
    for j in range(3):
        for xx in range(4):
            at = pl.multiple_of(zh * 1536 + xx * 384 + j * 128, 128)
            part = pl.ds(xx * 128, 128)
            loads.append(pltpu.make_async_copy(w_in_hbm.at[:, pl.ds(at, 128)], w_in.at[j, :, part], w_sem.at[0, j, xx]))
            loads.append(pltpu.make_async_copy(w_out_hbm.at[pl.ds(at, 128), :], w_out.at[j, part, :], w_sem.at[1, j, xx]))
    for load in loads:
        load.start()
    barrier = pltpu.get_barrier_semaphore()
    for target in targets.values():
        pl.semaphore_signal(barrier, inc=1, device_id=target, device_id_type=MESH)
    pl.semaphore_wait(barrier, len(targets))

    def place(a, q, at, first=0, rows=192):
        at = lax.rem(at + 16, 8)
        row = pl.multiple_of(lax.rem(at, 4) * 192 + first, 32)
        return act.at[a, q, pl.ds(row, rows), pl.ds(pl.multiple_of((at // 4) * 128, 128), 128)]

    def gather(a, q):
        source = (tok_in, cot_in)[a]

        def begin():
            place(a, q, z)[...] = source[:, pl.ds(q * 128, 128)]

        n = lambda *rest: ("g", a, q) + rest
        if (a, q) in FAR_GATHERS:
            for sign, d in ((1, "z+"), (-1, "z-")):
                near, far, half = z - sign, z - 2 * sign, (0 if sign == 1 else 96, 96)
                plan.copy(n(0, d), d + d[1], place(a, q, z), place(a, q, z), place(a, q, far))
                plan.copy(n(1, d), d, place(a, q, z), place(a, q, z), place(a, q, near))
                plan.copy(n(2, d), d + d[1], place(a, q, far, *half), place(a, q, far, *half), place(a, q, z - 4 * sign, *half))
                plan.copy(n(3, d), d, place(a, q, far), place(a, q, far), place(a, q, z - 3 * sign))
            plan.step(n(0), [], begin, [n(s, d) for s in (0, 1) for d in ("z+", "z-")])
            plan.step(n(1), [n(0, d) for d in ("z+", "z-")], None, [n(s, d) for s in (2, 3) for d in ("z+", "z-")])
            plan.step(("act", a, q), [n(s, d) for s in (1, 2, 3) for d in ("z+", "z-")], None)
            return
        for s in range(4):
            for sign, d in ((1, "z+"), (-1, "z-")):
                first, rows = (0, 192) if s < 3 else ((0, 96) if sign == 1 else (96, 96))
                here = place(a, q, z - sign * s, first, rows)
                there = place(a, q, z - sign * (s + 1), first, rows)
                plan.copy(n(s, d), d, here, here, there)
            needs = [n(s - 1, d) for d in ("z+", "z-")] if s else []
            plan.step(n(s), needs, begin if s == 0 else None, [n(s, d) for d in ("z+", "z-")])
        plan.step(("act", a, q), [n(3, d) for d in ("z+", "z-")], None)

    for a in range(2):
        for q in range(4):
            gather(a, q)

    def wait_weights():
        for load in loads:
            load.wait()

    plan.step("weights", [], wait_weights)

    def hidden_task(t):
        p, q0, nq, j0, nj = TASKS[t]
        units = [(q, j) for q in range(q0, q0 + nq) for j in range(j0, j0 + nj)]
        cut = (p, pl.ds(q0, nq), pl.ds(j0, nj))

        def product(q, j, row):
            if p == 0:
                return dot(w_in[j, :, pl.ds(row, 256)], act[0, q], (0, 0))
            return dot(w_out[j, pl.ds(row, 256), :], act[1, q], (1, 0))

        def other_half():
            for q, j in units:
                csnd[p, q, j] = product(q, j, pl.multiple_of((1 - c) * 256, 256)).astype(BF)

        def own_half():
            for q, j in units:
                own[q, j] = product(q, j, pl.multiple_of(c * 256, 256))

        def mine(q, j, rel, half):
            row = pl.ds(pl.multiple_of(lax.rem(y + rel, 4) * 64 + half * 32, 32), 32)
            return own[q, j, row, :] + crcv[p, q, j, row, :].astype(F32)

        def first_sums():
            for q, j in units:
                for rel, half in ((2, 0), (2, 1), (1, 1), (3, 0)):
                    ysnd[p, q, j, rel - 1, half] = mine(q, j, rel, half).astype(BF)

        def relay_sums():
            for q, j in units:
                for rel, half in ((1, 0), (3, 1)):
                    total = mine(q, j, rel, half) + yrcv[p, q, j, 1, half].astype(F32)
                    ysnd[p, q, j, rel - 1, half] = total.astype(BF)

        def activate():
            for q, j in units:
                for half in range(2):
                    total = mine(q, j, 0, half)
                    total = total + yrcv[p, q, j, 0, half].astype(F32) + yrcv[p, q, j, 2, half].astype(F32)
                    keep = pl.ds(half * 32, 32)
                    if p == 0:
                        value, slope = gelu_parts(total)
                        deriv[q, j, keep, :] = slope
                    else:
                        value = total * deriv[q, j, keep, :]
                    row = pl.ds(pl.multiple_of(c * 256 + y * 64 + half * 32, 32), 32)
                    hid[p, q, j, row, :] = value.astype(BF)

        def piece(core, rel, first=0, rows=64):
            row = core * 256 + lax.rem(y + rel, 4) * 64 + first
            return hid.at[(*cut, pl.ds(pl.multiple_of(row, 32), rows))]

        n = lambda *rest: ("h", t) + rest
        plan.copy(n("c"), "c", csnd.at[cut], crcv.at[cut], crcv.at[cut])
        for rel, half, d in ((2, 0, "y+"), (2, 1, "y-"), (1, 1, "y+"), (3, 0, "y-"), (1, 0, "y+"), (3, 1, "y-")):
            src, dst = ysnd.at[(*cut, rel - 1, half)], yrcv.at[(*cut, rel - 1, half)]
            plan.copy(n("r", rel, half), d, src, dst, dst)
        plan.step(n("other"), [("act", p, q) for q in range(q0, q0 + nq)] + ["weights"], other_half, [n("c")])
        plan.step(n("own"), [n("other")], own_half)
        plan.step(n("first"), [n("own"), n("c")], first_sums, [n("r", 2, 0), n("r", 2, 1), n("r", 1, 1), n("r", 3, 0)])
        plan.step(n("relay"), [n("first"), n("r", 2, 0), n("r", 2, 1)], relay_sums, [n("r", 1, 0), n("r", 3, 1)])
        plan.copy(n("a", "+"), "y+", piece(c, 0), piece(c, 0), piece(c, 3))
        plan.copy(n("a", "-"), "y-", piece(c, 0), piece(c, 0), piece(c, 1))
        far = t in FAR_HIDDEN
        for sign, rel, first in (("+", 3, 0), ("-", 1, 32)):
            here = piece(c, 0 if far else rel, first, 32)
            plan.copy(n("f", sign), "y2" if far else "y" + sign, here, here, piece(c, 2, first, 32))
        for rel in range(4):
            plan.copy(n("k", rel), "c", piece(c, rel), piece(c, rel), piece(1 - c, rel))
        plan.step(n("act"), [n("relay")] + [n("r", *k) for k in ((1, 1), (3, 0), (1, 0), (3, 1))], activate, [n("a", "+"), n("a", "-")] + [n("f", "+"), n("f", "-")] * far + [n("k", 0)])
        if far:
            plan.step(n("pass"), [n(a, b) for a in "af" for b in "+-"], None, [n("k", 1), n("k", 3), n("k", 2)])
        else:
            plan.step(n("pass"), [n("a", "+"), n("a", "-")], None, [n("f", "+"), n("f", "-"), n("k", 1), n("k", 3)])
            plan.step(n("last"), [n("f", "+"), n("f", "-")], None, [n("k", 2)])
        plan.step(n("done"), [n("k", rel) for rel in range(4)], None)

    for t in range(len(TASKS)):
        hidden_task(t)

    def hidden_ready(p, keep):
        return [("h", t, "done") for t, task in enumerate(TASKS) if task[0] == p and keep(*task[1:])]

    def gradient(p, j):
        other = 1 - p
        slot = p * 3 + j

        def multiply():
            xtmp[...] = sum(dot(hid[p, q, j], act[other, q], (1, 1)) for q in range(4))
            for to in range(4):
                for half in range(2):
                    xsnd[slot, to, half] = xtmp[pl.ds(to * 128 + half * 64, 64), :].astype(BF)
            xown[slot] = xtmp[pl.ds(pl.multiple_of(x * 128, 128), 128), :]

        def relay_sums():
            for rel, half in ((1, 0), (3, 1)):
                to = lax.rem(x + rel, 4)
                total = xsnd[slot, to, half].astype(F32) + xrcv[slot, 1, half].astype(F32)
                xsnd[slot, to, half] = total.astype(BF)

        def finish():
            for half in range(2):
                rows = pl.ds(half * 64, 64)
                xown[slot, rows, :] = xown[slot, rows, :] + xrcv[slot, 0, half].astype(F32) + xrcv[slot, 2, half].astype(F32)
            if p == 0:
                gout_out[pl.ds(j * 128, 128), :] = xown[slot].astype(BF)
            else:
                gin_out[:, pl.ds(j * 128, 128)] = xown[slot].T.astype(BF)

        n = lambda *rest: ("w", p, j) + rest
        for rel, half, d in ((2, 0, "x+"), (2, 1, "x-"), (1, 1, "x+"), (3, 0, "x-"), (1, 0, "x+"), (3, 1, "x-")):
            there = xrcv.at[slot, rel - 1, half]
            plan.copy(n("r", rel, half), d, xsnd.at[slot, lax.rem(x + rel, 4), half], there, there)
        needs = [("act", other, q) for q in range(4)] + hidden_ready(p, lambda q0, nq, j0, nj: j0 <= j < j0 + nj)
        plan.step(n("mul"), needs, multiply, [n("r", 2, 0), n("r", 2, 1), n("r", 1, 1), n("r", 3, 0)])
        plan.step(n("relay"), [n("mul"), n("r", 2, 0), n("r", 2, 1)], relay_sums, [n("r", 1, 0), n("r", 3, 1)])
        plan.step(n("end"), [n("r", *k) for k in ((1, 1), (3, 0), (1, 0), (3, 1))], finish)

    for p in range(2):
        for j in range(3):
            gradient(p, j)

    def result(p, q0, nq):
        qs, cut = range(q0, q0 + nq), pl.ds(q0, nq)

        def multiply():
            for q in qs:
                if p == 0:
                    zacc[p, q] = sum(dot(w_out[j], hid[0, q, j], (0, 0)) for j in range(3))
                else:
                    zacc[p, q] = sum(dot(w_in[j], hid[1, q, j], (1, 0)) for j in range(3))

        def mine(q, rel, first=0, rows=192):
            at = lax.rem(z + rel + 8, 8)
            row = pl.multiple_of(lax.rem(at, 4) * 192 + first, 32)
            return zacc[p, q, pl.ds(row, rows), pl.ds(pl.multiple_of((at // 4) * 128, 128), 128)]

        def first():
            for q in qs:
                zsnd[p, q, 0, 0, pl.ds(0, 96), :] = mine(q, 4, 0, 96).astype(BF)
                zsnd[p, q, 1, 0, pl.ds(96, 96), :] = mine(q, 4, 96, 96).astype(BF)

        def add(s):
            def body():
                for q in qs:
                    for d, rel in ((0, 4 - s), (1, 4 + s)):
                        for half in range(2):
                            total = mine(q, rel, half * 96, 96)
                            rows = pl.ds(half * 96, 96)
                            if s > 1 or half == d:
                                total = total + zrcv[p, q, d, s - 1, rows, :].astype(F32)
                            zsnd[p, q, d, s, rows, :] = total.astype(BF)

            return body

        def first_far():
            first()
            for q in qs:
                for d, sign in ((0, 1), (1, -1)):
                    zsnd[p, q, d, 1] = mine(q, 3 * sign).astype(BF)
                    zsnd[p, q, d, 3] = mine(q, sign).astype(BF)

        def add_far():
            for q in qs:
                for d, sign in ((0, 1), (1, -1)):
                    for half in range(2):
                        rows = pl.ds(half * 96, 96)
                        total = mine(q, 2 * sign, half * 96, 96) + zrcv[p, q, d, 1, rows, :].astype(F32)
                        if half == d:
                            total = total + zrcv[p, q, d, 0, rows, :].astype(F32)
                        zsnd[p, q, d, 2, rows, :] = total.astype(BF)

        is_far = (p, q0) in FAR_SUMS

        def finish():
            for q in qs:
                total = mine(q, 0)
                for d in range(2):
                    total = total + zrcv[p, q, d, 3].astype(F32)
                    if is_far:
                        total = total + zrcv[p, q, d, 2].astype(F32)
                (mix_out, dtok_out)[p][:, pl.ds(q * 128, 128)] = total.astype(BF)

        n = lambda *rest: ("z", p, q0) + rest
        for d, link in ((0, "z+"), (1, "z-")):
            for s in range(4):
                rows = pl.ds(0, 192) if s else pl.ds(d * 96, 96)
                there = zrcv.at[p, cut, d, s, rows]
                way = link + link[1] if is_far and s in (0, 2) else link
                plan.copy(n("r", s, d), way, zsnd.at[p, cut, d, s, rows], there, there)
        needs = hidden_ready(p, lambda a0, na, j0, nj: a0 < q0 + nq and q0 < a0 + na)
        plan.step(n("mul"), needs, multiply)
        if is_far:
            plan.step(n(0), [n("mul")], first_far, [n("r", s, d) for s in (0, 1, 3) for d in range(2)])
            plan.step(n(1), [n("r", s, d) for s in (0, 1) for d in range(2)], add_far, [n("r", 2, 0), n("r", 2, 1)])
            plan.step(n("end"), [n("r", s, d) for s in (2, 3) for d in range(2)], finish)
            return
        plan.step(n(0), [n("mul")], first, [n("r", 0, 0), n("r", 0, 1)])
        for s in range(1, 4):
            plan.step(n(s), [n("r", s - 1, 0), n("r", s - 1, 1)], add(s), [n("r", s, 0), n("r", s, 1)])
        plan.step(n("end"), [n("r", 3, 0), n("r", 3, 1)], finish)

    for p in range(2):
        for q0, nq in SUMS[p]:
            result(p, q0, nq)

    index = {name: i for i, name in enumerate(plan.copies)}
    waited, sent = set(), []

    def remote(name, landing):
        link, src, dst, there = plan.copies[name]
        i = index[name]
        src, dst = (there, there) if landing else (src, dst)
        return pltpu.make_async_remote_copy(src, dst, send_sem.at[i], recv_sem.at[i], device_id=targets[link], device_id_type=MESH)

    names = list(plan.steps)
    for i in ORDER:
        name = names[i]
        needs, body, sends = plan.steps[name]
        for need in needs:
            if need in plan.copies and need not in waited:
                remote(need, True).wait_recv()
                waited.add(need)
        if body is not None:
            body()
        for copy in sends:
            remote(copy, False).start()
            sent.append(copy)
        while len(sent) > 40:
            remote(sent.pop(0), False).wait_send()
    for copy in sent:
        remote(copy, False).wait_send()


def copies_in_all():
    return 64 + 15 * len(TASKS) + 36 + 8 * sum(len(groups) for groups in SUMS)


def hand_over(*refs):
    for i in range(4):
        refs[4 + i][...] = refs[i][...]


def per_device(tokens, w_in, w_out, cotangent):
    vmem, far = pl.BlockSpec(memory_space=pltpu.VMEM), pl.BlockSpec(memory_space=pl.ANY)
    copies = copies_in_all()
    shapes = [jax.ShapeDtypeStruct(s, BF) for s in ((192, 512), (192, 512), (768, 384), (384, 768))]
    results = pl.pallas_call(
        kernel,
        out_shape=shapes,
        in_specs=[vmem, vmem, far, far],
        out_specs=[vmem] * 4,
        scratch_shapes=[
            pltpu.VMEM((2, 4, 768, 256), BF),
            pltpu.VMEM((3, 768, 512), BF),
            pltpu.VMEM((3, 512, 768), BF),
            pltpu.SemaphoreType.DMA((2, 3, 4)),
            pltpu.VMEM((2, 4, 3, 256, 256), BF),
            pltpu.VMEM((2, 4, 3, 256, 256), BF),
            pltpu.VMEM((4, 3, 256, 256), F32),
            pltpu.VMEM((2, 4, 3, 3, 2, 32, 256), BF),
            pltpu.VMEM((2, 4, 3, 3, 2, 32, 256), BF),
            pltpu.VMEM((4, 3, 64, 256), F32),
            pltpu.VMEM((2, 4, 3, 512, 256), BF),
            pltpu.VMEM((6, 4, 2, 64, 768), BF),
            pltpu.VMEM((6, 3, 2, 64, 768), BF),
            pltpu.VMEM((6, 128, 768), F32),
            pltpu.VMEM((512, 768), F32),
            pltpu.VMEM((2, 4, 768, 256), F32),
            pltpu.VMEM((2, 4, 2, 4, 192, 128), BF),
            pltpu.VMEM((2, 4, 2, 4, 192, 128), BF),
            pltpu.SemaphoreType.DMA((copies,)),
            pltpu.SemaphoreType.DMA((copies,)),
        ],
        compiler_params=pltpu.CompilerParams(
            collective_id=0, has_side_effects=True, vmem_limit_bytes=62 * 2**20
        ),
        cost_estimate=pl.CostEstimate(flops=14_500_000_000, bytes_accessed=12_000_000, transcendentals=400_000),
    )(tokens.T, cotangent.T, w_in, w_out)

    mixed, d_tokens, grad_in, grad_out = pl.pallas_call(
        hand_over,
        out_shape=shapes,
        in_specs=[vmem] * 4,
        out_specs=[vmem] * 4,
    )(*results)
    return (mixed.T, d_tokens.T, grad_in, grad_out)


def solution(mesh):
    split = Mesh(mesh.devices.reshape(2, 4, 4, 4, 2), ("zh", "x", "zl", "y", "c"))
    rows = P(("zh", "x"), ("y", "c", "zl"))
    return jax.shard_map(
        per_device,
        mesh=split,
        in_specs=(rows, P(("y", "c"), "zl"), P("zl", ("y", "c")), rows),
        out_specs=(rows, rows, P(("y", "c"), ("zl", "zh", "x")), P(("zl", "zh", "x"), ("y", "c"))),
        check_vma=False,
    )
```
